32 devices in a mesh: slab: 8 (over y, x, core), view: 4 (over z).
Axes of the slice: x: 2, y: 2, z: 4, core: 2. Of those that a mesh axis runs over, the one named last changes fastest.
Arguments:
- volume: float32 [8, 64, 4096], P('view', 'slab'), may hold values from -6 to 6
- vox_inv: float32 [8, 64, 4096], P('view', 'slab'), may hold values from 0.01 to 0.1
- measured: float32 [128, 12, 4096], P('slab', 'view'), may hold values from -24 to 24
- ray_inv: float32 [128, 12, 4096], P('slab', 'view'), may hold values from 0.05 to 0.5
- col_shift: int32 [12, 8], replicated, may hold values from -512 to 512
- col_frac: float32 [12, 8], replicated, may hold values from 0 to 1
- row_offset: int32 [12, 64], P('view', 'slab'), may hold values from -8 to 8, as said below
- row_frac: float32 [12, 64], P('view', 'slab'), may hold values from 0 to 1
Outputs:
- updated: float32 [8, 64, 4096], P('view', 'slab')
- residual: bfloat16 [128, 12, 4096], P('slab', 'view')
The draws below stay inside these ranges and needn't reach their ends.
Inputs may be any that keep to these rules, and one draw needn't show every extreme that they name: `row_offset`: every entry lies in -8 to 8, and both ends occur.
All inputs are finite; a program needn't handle non-finite values.
Results may differ from the reference program's by a relative error of at most 0.0095.
Values may be sent and summed in bfloat16 or wider, within the bound.
A program may use at most 64 MiB of HBM per device.

```python
import math
import jax
import jax.numpy as jnp
from jax import lax

COLS = 4096
Z_DEV = 8
ROW_DEV = 16
Y = 8
Z = 64
ROWS = 128
VIEWS = 12
N_SLAB = 8


def draw_row_offset(key, part):
    half = ROW_DEV // 2
    values = jax.random.randint(key, (VIEWS, Z), -half, half + 1)
    values = values.at[0, 0].set(-half)
    values = values.at[VIEWS - 1, Z - 1].set(half)
    return values.astype(jnp.int32)


def place_ends(entries, own_key, low, top_value):
    index_at = [jax.random.randint(jax.random.fold_in(own_key, axis), (), 0, length) for axis, length in enumerate(entries.shape)]
    longest = entries.shape.index(max(entries.shape))
    next_to = index_at[:longest] + [(index_at[longest] + 1) % entries.shape[longest]] + index_at[longest + 1:]
    return entries.at[tuple(index_at)].set(low).at[tuple(next_to)].set(top_value)


def steps_of(own_key, extent, pieces, smallest, high):
    gain, own = 1.0, jax.random.fold_in(own_key, 6)
    for dim, shards_of in pieces:
        draws = jnp.exp(jax.random.uniform(jax.random.fold_in(own, dim), (shards_of,), jnp.float32, smallest / len(pieces), high / len(pieces)))
        gain = gain * jnp.repeat(draws, extent[dim] // shards_of).reshape([-1 if axis == dim else 1 for axis in range(len(extent))])
    return gain


def noise(key, shape, scale, bound, split=(), kind=jnp.bfloat16):
    factor_of = steps_of(key, shape, split, -0.22, 0.18) if split else 1.0
    drawn = jax.random.normal(key, shape, jnp.float32) * scale * factor_of
    return jnp.minimum(jnp.maximum(drawn, -bound), bound).astype(kind)


def setup_inputs(seed: int = 0) -> dict:
    seeds = jax.random.split(jax.random.key(seed), 9)
    volume = noise(seeds[0], (Y, Z, COLS), 1.0, 6.0, ((0, 4), (1, 8)), jnp.float32)
    vox_inv = jnp.clip(jnp.exp(math.log(0.1) - 2.3025851 * jax.random.uniform(seeds[1], (Y, Z, COLS), jnp.float32) ** steps_of(seeds[1], (Y, Z, COLS), ((0, 4), (1, 8)), -0.2, 0.2)), 0.01, 0.1)
    measured = noise(seeds[2], (ROWS, VIEWS, COLS), 4.0, 24.0, ((0, 8), (1, 4)), jnp.float32)
    ray_inv = jnp.clip(jnp.exp(math.log(0.5) - 2.3025851 * jax.random.uniform(seeds[3], (ROWS, VIEWS, COLS), jnp.float32) ** steps_of(seeds[3], (ROWS, VIEWS, COLS), ((0, 8), (1, 4)), -0.2, 0.2)), 0.05, 0.5)
    col_shift = place_ends(jax.random.randint(seeds[4], (VIEWS, Y), -(COLS // 8), COLS // 8 + 1), jax.random.fold_in(seeds[4], 1), -(COLS // 8), (COLS // 8 + 1) - 1).astype(jnp.int32)
    col_frac = jnp.clip(jax.random.uniform(seeds[5], (VIEWS, Y), jnp.float32, 0.0, 1.0), 0.0, 1.0)
    row_offset = draw_row_offset(jax.random.fold_in(seeds[8], 71), 0)
    row_frac = jnp.clip(1.0 * jax.random.uniform(seeds[7], (VIEWS, Z), jnp.float32) ** steps_of(seeds[7], (VIEWS, Z), ((0, 4), (1, 8)), -0.2, 0.2), 0.0, 1.0)
    return {"volume": volume, "vox_inv": vox_inv, "measured": measured, "ray_inv": ray_inv, "col_shift": col_shift, "col_frac": col_frac, "row_offset": row_offset, "row_frac": row_frac}


def band_rows(base, frac, rows):
    r = rows[None, :, None]
    first = jnp.where(r == base[:, None, :], 1.0 - frac[:, None, :], 0.0)
    second = jnp.where(r == base[:, None, :] + 1, frac[:, None, :], 0.0)
    return (first + second).astype(jnp.float32)


def shear_forward(lines, shift, frac):
    width = lines.shape[2]
    cols = jnp.arange(width, dtype=jnp.int32)
    first = cols[None, :] + shift[:, None]
    second = first + 1
    weight_a = jnp.where((first >= 0) & (first < width), 1.0 - frac[:, None], 0.0)
    weight_b = jnp.where((second >= 0) & (second < width), frac[:, None], 0.0)
    index_a = jnp.broadcast_to(jnp.clip(first, 0, width - 1)[:, None, :], lines.shape)
    index_b = jnp.broadcast_to(jnp.clip(second, 0, width - 1)[:, None, :], lines.shape)
    taken_a = jnp.take_along_axis(lines, index_a, axis=2).astype(jnp.float32)
    taken_b = jnp.take_along_axis(lines, index_b, axis=2).astype(jnp.float32)
    return jnp.sum(taken_a * weight_a[:, None, :] + taken_b * weight_b[:, None, :], axis=0)


def shear_back(image, shift, frac):
    count = shift.shape[0]
    width = image.shape[1]
    cols = jnp.arange(width, dtype=jnp.int32)
    first = cols[None, :] - shift[:, None]
    second = first - 1
    weight_a = jnp.where((first >= 0) & (first < width), 1.0 - frac[:, None], 0.0)
    weight_b = jnp.where((second >= 0) & (second < width), frac[:, None], 0.0)
    spread = jnp.broadcast_to(image[None], (count,) + image.shape)
    index_a = jnp.broadcast_to(jnp.clip(first, 0, width - 1)[:, None, :], spread.shape)
    index_b = jnp.broadcast_to(jnp.clip(second, 0, width - 1)[:, None, :], spread.shape)
    taken_a = jnp.take_along_axis(spread, index_a, axis=2).astype(jnp.float32)
    taken_b = jnp.take_along_axis(spread, index_b, axis=2).astype(jnp.float32)
    return taken_a * weight_a[:, None, :] + taken_b * weight_b[:, None, :]


def reference(volume, vox_inv, measured, ray_inv, col_shift, col_frac, row_offset, row_frac):
    lines = volume.astype(jnp.bfloat16)
    sheared = lax.map(lambda item: shear_forward(lines, item[0], item[1]), (col_shift, col_frac))
    z_all = jnp.arange(Z, dtype=jnp.int32)
    base = (z_all[None, :] * ROW_DEV) // Z_DEV + row_offset
    band = band_rows(base, row_frac, jnp.arange(ROWS, dtype=jnp.int32))

    def add_slab(k, total):
        band_k = lax.dynamic_slice_in_dim(band, k * Z_DEV, Z_DEV, 2)
        sheared_k = lax.dynamic_slice_in_dim(sheared, k * Z_DEV, Z_DEV, 1)
        part = jnp.einsum("vrz,vzc->rvc", band_k, sheared_k, precision=lax.Precision.HIGHEST)
        part = lax.optimization_barrier(part.astype(jnp.bfloat16))
        return total + part.astype(jnp.float32)

    projected = lax.fori_loop(0, N_SLAB, add_slab, jnp.zeros((ROWS, VIEWS, COLS), jnp.float32))
    residual = (ray_inv * (measured - projected)).astype(jnp.bfloat16)
    images = jnp.einsum("vrz,rvc->vzc", band, residual.astype(jnp.float32), precision=lax.Precision.HIGHEST).astype(jnp.bfloat16)

    def add_view(view, total):
        image = lax.dynamic_index_in_dim(images, view, 0, keepdims=False)
        shift = lax.dynamic_index_in_dim(col_shift, view, 0, keepdims=False)
        frac = lax.dynamic_index_in_dim(col_frac, view, 0, keepdims=False)
        return total + shear_back(image, shift, frac)

    back = lax.fori_loop(0, VIEWS, add_view, jnp.zeros((Y, Z, COLS), jnp.float32))
    return volume + vox_inv * back, residual
```

```python
import functools

import jax
import jax.numpy as jnp
from jax import lax
from jax.experimental import pallas as pl
from jax.experimental.pallas import tpu as pltpu
from jax.sharding import PartitionSpec as P

F32 = jnp.float32
BF16 = jnp.bfloat16
LANES = 128


def dot(a, b):
    return jnp.dot(a, b, preferred_element_type=F32)


def kernel(
    sizes, vol, vox, meas, ray, shift, frac, off, rfrac, upd, res,
    gat, lines, taps_f, taps_b, acc, sheared, meta, resid, img_out, img_in, images, back_out, back_in,
    ag_send, ag_recv, me_send, me_recv, sh_send, sh_recv, im_send, im_recv, rs_send, rs_recv,
):
    n_view, n_slab, views, z_dev, row_dev, width = sizes
    half = width // 2
    margin = (lines.shape[1] * LANES - half) // 2
    blocks = half // LANES
    n_lines = 2 * n_view
    me = lax.axis_index("view")
    slab = lax.axis_index("slab")
    has_lo = slab > 0
    has_hi = slab < n_slab - 1

    def ag_copy(k):
        dest = lax.rem(me + k, n_view)
        return pltpu.make_async_remote_copy(
            gat.at[me], gat.at[me], ag_send.at[k], ag_recv.at[me], device_id={"view": dest}
        )

    def ag_arrival(src):
        return pltpu.make_async_remote_copy(
            gat.at[src], gat.at[src], ag_send.at[0], ag_recv.at[src], device_id={"view": src}
        )

    def rs_copy(k):
        dest = lax.rem(me + k, n_view)
        return pltpu.make_async_remote_copy(
            back_out.at[dest], back_in.at[me], rs_send.at[k], rs_recv.at[me], device_id={"view": dest}
        )

    def rs_arrival(src):
        return pltpu.make_async_remote_copy(
            back_out.at[src], back_in.at[src], rs_send.at[0], rs_recv.at[src], device_id={"view": src}
        )

    def halo(own, slots, send, recv, side, low_slot, high_slot):
        slot = high_slot if side == 0 else low_slot
        return pltpu.make_async_remote_copy(
            own, slots.at[slot], send.at[side], recv.at[1 - side],
            device_id={"slab": slab - 1 if side == 0 else slab + 1},
        )

    sides = ((0, has_lo), (1, has_hi))

    def meta_copy(side):
        return halo(meta.at[1], meta, me_send, me_recv, side, 0, 2)

    def sheared_copy(side):
        return halo(sheared.at[1], sheared, sh_send, sh_recv, side, 0, 2)

    def image_copy(side):
        return halo(img_out.at[side], img_in, im_send, im_recv, side, 0, 1)

    barrier = pltpu.get_barrier_semaphore()

    def greet(k, _):
        pl.semaphore_signal(barrier, inc=1, device_id={"view": lax.rem(me + k, n_view)})
        return 0

    lax.fori_loop(1, n_view, greet, 0)
    for side, has in sides:
        @pl.when(has)
        def _():
            pl.semaphore_signal(barrier, inc=1, device_id={"slab": slab - 1 if side == 0 else slab + 1})

    gat[me] = vol[...].reshape(2 * z_dev, width).astype(BF16)

    lane = lax.broadcasted_iota(jnp.int32, (8, LANES), 1)
    offs = jnp.zeros((8, LANES), F32)
    fracs = jnp.zeros((8, LANES), F32)
    for v in range(views):
        for z in range(z_dev):
            here = (lane // 16 == v) & (lane % 8 == z)
            offs = jnp.where(here, off[v, z].astype(F32), offs)
            fracs = jnp.where(here, rfrac[v, z], fracs)
    meta[1, 0:8] = offs
    meta[1, 8:16] = fracs

    peers = n_view + 1 - (slab == 0).astype(jnp.int32) - (slab == n_slab - 1).astype(jnp.int32)
    pl.semaphore_wait(barrier, peers)

    def send_lines(k, _):
        ag_copy(k).start()
        return 0

    lax.fori_loop(1, n_view, send_lines, 0)
    for side, has in sides:
        @pl.when(has)
        def _():
            meta_copy(side).start()

        @pl.when(jnp.logical_not(has))
        def _():
            slot = 0 if side == 0 else 2
            meta[slot] = jnp.zeros(meta.shape[1:], F32)
            sheared[slot] = jnp.zeros(sheared.shape[1:], BF16)
            img_in[side] = jnp.zeros(img_in.shape[1:], BF16)

    delta = lax.broadcasted_iota(jnp.int32, (2 * LANES, LANES), 0) - lax.broadcasted_iota(
        jnp.int32, (2 * LANES, LANES), 1
    )

    def place(s):
        whole = lax.shift_right_arithmetic(s, 7)
        return whole, s - whole * LANES

    def taps(s, first, second):
        _, r = place(s)
        return jnp.where(delta == r, first, jnp.where(delta == r + 1, second, 0.0)).astype(BF16)

    def build(y, _):
        for v in range(views):
            s = shift[me * views + v, y]
            f = frac[me * views + v, y]
            taps_f[v * n_lines + y] = taps(s, 1.0 - f, f)
            taps_b[v * n_lines + y] = taps(-s - 1, f, 1.0 - f)
        return 0

    lax.fori_loop(0, n_lines, build, 0)

    def put(ref, at, low, high):
        zeros = jnp.zeros((z_dev, margin), F32)
        top = jnp.concatenate([zeros, low, high[:, :margin]], axis=1)
        bottom = jnp.concatenate([low[:, half - margin :], high, zeros], axis=1)
        both = jnp.concatenate([top, bottom], axis=0).astype(BF16)
        for b in range(both.shape[1] // LANES):
            ref[at, b] = both[:, b * LANES : (b + 1) * LANES]

    def windows(ref, at, s):
        whole, _ = place(s)
        taken = ref[at, pl.ds(margin // LANES + whole, blocks + 1)]
        taken = taken.reshape((blocks + 1) * 16, LANES)
        return jnp.concatenate([taken[:-16], taken[16:]], axis=1)

    acc[...] = jnp.zeros(acc.shape, F32)

    def project(k, _):
        src = lax.rem(me + k, n_view)

        @pl.when(k > 0)
        def _():
            ag_arrival(src).wait_recv()

        for l in range(2):
            y = 2 * src + l
            x = gat[src].astype(F32)[l * z_dev : (l + 1) * z_dev]
            put(lines, y, x[:, :half], x[:, half:])
            for v in range(views):
                s = shift[me * views + v, y]
                acc[v] += dot(windows(lines, y, s), taps_f[v * n_lines + y])
        return 0

    lax.fori_loop(0, n_view, project, 0)
    for v in range(views):
        for b in range(blocks):
            sheared[1, 16 * v : 16 * (v + 1), b * LANES : (b + 1) * LANES] = acc[
                v, 16 * b : 16 * (b + 1)
            ].astype(BF16)

    for side, has in sides:
        @pl.when(has)
        def _():
            sheared_copy(side).start()

    rows = 2 * views * row_dev
    row = lax.broadcasted_iota(jnp.int32, (rows, LANES), 0)
    col = lax.broadcasted_iota(jnp.int32, (rows, LANES), 1)
    same = ((row // (views * row_dev)) == (col // 8) % 2) & ((row // row_dev) % views == col // 16)
    above_slice = (row % row_dev - (col % 8) * row_dev // z_dev).astype(F32)

    def weights(slot):
        past = above_slice - (meta[slot, 0:1] + float((slot - 1) * row_dev)) - meta[slot, 8:9]
        return jnp.where(same, jnp.maximum(1.0 - jnp.abs(past), 0.0), 0.0)

    for side, has in sides:
        @pl.when(has)
        def _():
            meta_copy(1 - side).wait_recv()

    keep = 2 * views * z_dev
    own = weights(1)
    below = weights(0)
    above = weights(2)
    proj = dot(own[:, :keep].astype(BF16), sheared[1])
    for side, has in sides:
        @pl.when(has)
        def _():
            sheared_copy(1 - side).wait_recv()
    proj += dot(below[:, :keep].astype(BF16), sheared[0])
    proj += dot(above[:, :keep].astype(BF16), sheared[2])

    for h in range(2):
        for v in range(views):
            at = slice(h * half, (h + 1) * half)
            lo = (h * views + v) * row_dev
            value = (ray[v, :, at] * (meas[v, :, at] - proj[lo : lo + row_dev])).astype(BF16)
            res[v, :, at] = value
            resid[lo : lo + row_dev] = value

    img_out[0] = dot(below.T[:keep].astype(BF16), resid[...]).astype(BF16)
    img_out[1] = dot(above.T[:keep].astype(BF16), resid[...]).astype(BF16)
    for side, has in sides:
        @pl.when(has)
        def _():
            image_copy(side).start()
    mine = dot(own.T[:keep].astype(BF16), resid[...])
    for side, has in sides:
        @pl.when(has)
        def _():
            image_copy(1 - side).wait_recv()
    mine += img_in[0].astype(F32) + img_in[1].astype(F32)
    for v in range(views):
        put(images, v, mine[16 * v : 16 * v + 8], mine[16 * v + 8 : 16 * v + 16])

    def spread(k, _):
        dest = lax.rem(me + k, n_view)
        for l in range(2):
            y = 2 * dest + l
            total = jnp.zeros((blocks * 16, LANES), F32)
            for v in range(views):
                s = -shift[me * views + v, y] - 1
                total += dot(windows(images, v, s), taps_b[v * n_lines + y])
            total = total.astype(BF16)
            for b in range(blocks):
                back_out[dest, 16 * l : 16 * (l + 1), b * LANES : (b + 1) * LANES] = total[
                    16 * b : 16 * (b + 1)
                ]

        @pl.when(k < n_view)
        def _():
            rs_copy(k).start()

        return 0

    lax.fori_loop(1, n_view + 1, spread, 0)

    for l in range(2):
        for h in range(2):
            at = slice(h * half, (h + 1) * half)
            rows_at = slice(16 * l + 8 * h, 16 * l + 8 * h + 8)
            acc_at = back_out[me, 16 * l : 16 * l + 16].astype(F32)[8 * h : 8 * h + 8]
            upd[l, :, at] = acc_at

    def collect(k, _):
        src = lax.rem(me + k, n_view)
        rs_arrival(src).wait_recv()
        for l in range(2):
            part = back_in[src, 16 * l : 16 * l + 16].astype(F32)
            for h in range(2):
                at = slice(h * half, (h + 1) * half)
                upd[l, :, at] += part[8 * h : 8 * h + 8]
        return 0

    lax.fori_loop(1, n_view, collect, 0)
    upd[...] = vol[...] + vox[...] * upd[...]

    def drain(k, _):
        ag_copy(k).wait_send()
        rs_copy(k).wait_send()
        return 0

    lax.fori_loop(1, n_view, drain, 0)
    for side, has in sides:
        @pl.when(has)
        def _():
            meta_copy(side).wait_send()
            sheared_copy(side).wait_send()
            image_copy(side).wait_send()


def per_device(volume, vox_inv, measured, ray_inv, col_shift, col_frac, row_offset, row_frac):
    y_dev, z_dev, width = volume.shape
    row_dev, views = measured.shape[:2]
    n_view, n_slab = lax.axis_size("view"), lax.axis_size("slab")
    half = width // 2
    margin = (width // 8 // LANES + 1) * LANES
    n_lines = n_view * y_dev
    packed = 2 * views * z_dev
    vmem = pl.BlockSpec(memory_space=pltpu.VMEM)
    smem = pl.BlockSpec(memory_space=pltpu.SMEM)
    dma = pltpu.SemaphoreType.DMA
    sizes = (n_view, n_slab, views, z_dev, row_dev, width)
    upd, res = pl.pallas_call(
        functools.partial(kernel, sizes),
        out_shape=[
            jax.ShapeDtypeStruct(volume.shape, F32),
            jax.ShapeDtypeStruct((views, row_dev, width), BF16),
        ],
        in_specs=[vmem] * 4 + [smem] * 4,
        out_specs=[vmem] * 2,
        scratch_shapes=[
            pltpu.VMEM((n_view, y_dev * z_dev, width), BF16),
            pltpu.VMEM((n_lines, (half + 2 * margin) // LANES, 2 * z_dev, LANES), BF16),
            pltpu.VMEM((views * n_lines, 2 * LANES, LANES), BF16),
            pltpu.VMEM((views * n_lines, 2 * LANES, LANES), BF16),
            pltpu.VMEM((views, half // LANES * 16, LANES), F32),
            pltpu.VMEM((3, packed, half), BF16),
            pltpu.VMEM((3, 16, LANES), F32),
            pltpu.VMEM((2 * views * row_dev, half), BF16),
            pltpu.VMEM((2, packed, half), BF16),
            pltpu.VMEM((2, packed, half), BF16),
            pltpu.VMEM((views, (half + 2 * margin) // LANES, 2 * z_dev, LANES), BF16),
            pltpu.VMEM((n_view, 2 * y_dev * z_dev, half), BF16),
            pltpu.VMEM((n_view, 2 * y_dev * z_dev, half), BF16),
            dma((n_view,)), dma((n_view,)),
            dma((2,)), dma((2,)),
            dma((2,)), dma((2,)),
            dma((2,)), dma((2,)),
            dma((n_view,)), dma((n_view,)),
        ],
        compiler_params=pltpu.CompilerParams(
            collective_id=0, has_side_effects=True, vmem_limit_bytes=48 * 1024 * 1024
        ),
    )(
        volume, vox_inv, measured.transpose(1, 0, 2), ray_inv.transpose(1, 0, 2),
        col_shift, col_frac, row_offset, row_frac,
    )
    return upd, res.transpose(1, 0, 2)


def solution(mesh):
    in_specs = (
        P("view", "slab", None),
        P("view", "slab", None),
        P("slab", "view", None),
        P("slab", "view", None),
        P(),
        P(),
        P("view", "slab"),
        P("view", "slab"),
    )
    out_specs = (P("view", "slab", None), P("slab", "view", None))
    return jax.shard_map(
        per_device, mesh=mesh, in_specs=in_specs, out_specs=out_specs, check_vma=False
    )
```

```python
import functools

import jax
import jax.numpy as jnp
from jax import lax
from jax.experimental import pallas as pl
from jax.experimental.pallas import tpu as pltpu
from jax.sharding import PartitionSpec as P

F32 = jnp.float32
BF16 = jnp.bfloat16
LANES = 128


def dot(a, b):
    return jnp.dot(a, b, preferred_element_type=F32)


def kernel(
    sizes, vol_at, vox_at, meas_at, ray_at, shift, frac, off, rfrac, upd, res,
    vol, vox, meas, ray,
    gat, lines, taps_f, taps_b, acc, sheared, sheared_out, sheared_in, meta, resid, img_out, img_in, images, back_out, back_in,
    ag_send, ag_recv, me_send, me_recv, sh_send, sh_recv, im_send, im_recv, rs_send, rs_recv, load_sem,
):
    n_view, n_slab, views, z_dev, row_dev, width = sizes
    half = width // 2
    margin = (lines.shape[1] * LANES - half) // 2
    blocks = half // LANES
    quarter = half // 2
    n_lines = 2 * n_view
    me = lax.axis_index("view")
    slab = lax.axis_index("slab")
    has_lo = slab > 0
    has_hi = slab < n_slab - 1

    loads = [
        pltpu.make_async_copy(src, dst, load_sem.at[i])
        for i, (src, dst) in enumerate(((vol_at, vol), (meas_at, meas), (ray_at, ray), (vox_at, vox)))
    ]
    loads[0].start()

    def ag_copy(k):
        dest = lax.rem(me + k, n_view)
        return pltpu.make_async_remote_copy(
            gat.at[me], gat.at[me], ag_send.at[k], ag_recv.at[me], device_id={"view": dest}
        )

    def ag_arrival(src):
        return pltpu.make_async_remote_copy(
            gat.at[src], gat.at[src], ag_send.at[0], ag_recv.at[src], device_id={"view": src}
        )

    def rs_copy(k):
        dest = lax.rem(me + k, n_view)
        return pltpu.make_async_remote_copy(
            back_out.at[dest], back_in.at[me], rs_send.at[k], rs_recv.at[me], device_id={"view": dest}
        )

    def rs_arrival(src):
        return pltpu.make_async_remote_copy(
            back_out.at[src], back_in.at[src], rs_send.at[0], rs_recv.at[src], device_id={"view": src}
        )

    def halo(own, slots, send, recv, side, low_slot, high_slot):
        slot = high_slot if side == 0 else low_slot
        return pltpu.make_async_remote_copy(
            own, slots.at[slot], send.at[side], recv.at[1 - side],
            device_id={"slab": slab - 1 if side == 0 else slab + 1},
        )

    sides = ((0, has_lo), (1, has_hi))

    def meta_copy(side):
        return halo(meta.at[3 + side], meta, me_send, me_recv, side, 0, 2)

    def sheared_copy(side):
        return halo(sheared_out.at[side], sheared_in, sh_send, sh_recv, side, 0, 1)

    def image_copy(side):
        return halo(img_out.at[side], img_in, im_send, im_recv, side, 0, 1)

    barrier = pltpu.get_barrier_semaphore()

    def greet(k, _):
        pl.semaphore_signal(barrier, inc=1, device_id={"view": lax.rem(me + k, n_view)})
        return 0

    lax.fori_loop(1, n_view, greet, 0)
    for side, has in sides:
        @pl.when(has)
        def _():
            pl.semaphore_signal(barrier, inc=1, device_id={"slab": slab - 1 if side == 0 else slab + 1})

    loads[0].wait()
    gat[me] = vol[...].reshape(2 * z_dev, width).astype(BF16)

    lane = lax.broadcasted_iota(jnp.int32, (8, LANES), 1)
    few = z_dev // 2
    slice_of = {1: lane % z_dev, 3: lane % few, 4: lane % few + few}
    for slot, slices in slice_of.items():
        offs = jnp.zeros((8, LANES), F32)
        fracs = jnp.zeros((8, LANES), F32)
        for v in range(views):
            for z in range(z_dev):
                here = (lane // 16 == v) & (slices == z)
                offs = jnp.where(here, off[v, z].astype(F32), offs)
                fracs = jnp.where(here, rfrac[v, z], fracs)
        meta[slot, 0:8] = offs
        meta[slot, 8:16] = fracs

    peers = n_view + 1 - (slab == 0).astype(jnp.int32) - (slab == n_slab - 1).astype(jnp.int32)
    pl.semaphore_wait(barrier, peers)

    def send_lines(k, _):
        ag_copy(k).start()
        return 0

    lax.fori_loop(1, n_view, send_lines, 0)
    for load in loads[1:]:
        load.start()
    for side, has in sides:
        @pl.when(has)
        def _():
            meta_copy(side).start()

        @pl.when(jnp.logical_not(has))
        def _():
            slot = 0 if side == 0 else 2
            meta[slot] = jnp.zeros(meta.shape[1:], F32)
            sheared_in[side] = jnp.zeros(sheared_in.shape[1:], BF16)
            img_in[side] = jnp.zeros(img_in.shape[1:], BF16)

    delta = lax.broadcasted_iota(jnp.int32, (2 * LANES, LANES), 0) - lax.broadcasted_iota(
        jnp.int32, (2 * LANES, LANES), 1
    )

    def place(s):
        whole = lax.shift_right_arithmetic(s, 7)
        return whole, s - whole * LANES

    def taps(s, first, second):
        _, r = place(s)
        return jnp.where(delta == r, first, jnp.where(delta == r + 1, second, 0.0)).astype(BF16)

    def build(y, _):
        for v in range(views):
            s = shift[y, me * views + v]
            f = frac[y, me * views + v]
            taps_f[v * n_lines + y] = taps(s, 1.0 - f, f)
            taps_b[v * n_lines + y] = taps(-s - 1, f, 1.0 - f)
        return 0

    lax.fori_loop(0, n_lines, build, 0)

    def put(ref, at, low, high):
        zeros = jnp.zeros((z_dev, margin), F32)
        top = jnp.concatenate([zeros, low, high[:, :margin]], axis=1)
        bottom = jnp.concatenate([low[:, half - margin :], high, zeros], axis=1)
        both = jnp.concatenate([top, bottom], axis=0).astype(BF16)
        for b in range(both.shape[1] // LANES):
            ref[at, b] = both[:, b * LANES : (b + 1) * LANES]

    def windows(ref, at, s):
        whole, _ = place(s)
        taken = ref[at, pl.ds(margin // LANES + whole, blocks + 1)]
        taken = taken.reshape((blocks + 1) * 16, LANES)
        return jnp.concatenate([taken[:-16], taken[16:]], axis=1)

    acc[...] = jnp.zeros(acc.shape, F32)

    def project(k, _):
        src = lax.rem(me + k, n_view)

        @pl.when(k > 0)
        def _():
            ag_arrival(src).wait_recv()

        for l in range(2):
            y = 2 * src + l
            x = gat[src].astype(F32)[l * z_dev : (l + 1) * z_dev]
            put(lines, y, x[:, :half], x[:, half:])
            for v in range(views):
                s = shift[y, me * views + v]
                acc[v] += dot(windows(lines, y, s), taps_f[v * n_lines + y])
        return 0

    lax.fori_loop(0, n_view, project, 0)
    low_rows = lax.broadcasted_iota(jnp.int32, (z_dev, LANES), 0) < few

    def turn(x):
        return pltpu.roll(x, few, 0)

    for v in range(views):
        for b in range(blocks // 2):
            first = acc[v, 16 * b : 16 * (b + 1)]
            second = acc[v, 16 * (b + blocks // 2) : 16 * (b + blocks // 2 + 1)]
            down, up = [], []
            for h in range(2):
                x, y = first[8 * h : 8 * h + 8], second[8 * h : 8 * h + 8]
                down.append(jnp.where(low_rows, x, turn(y)))
                up.append(jnp.where(low_rows, turn(x), y))
            at = (slice(16 * v, 16 * (v + 1)), slice(b * LANES, (b + 1) * LANES))
            sheared_out[(0,) + at] = jnp.concatenate(down, axis=0).astype(BF16)
            sheared_out[(1,) + at] = jnp.concatenate(up, axis=0).astype(BF16)

    for side, has in sides:
        @pl.when(has)
        def _():
            sheared_copy(side).start()

    for v in range(views):
        for b in range(blocks):
            sheared[16 * v : 16 * (v + 1), b * LANES : (b + 1) * LANES] = acc[
                v, 16 * b : 16 * (b + 1)
            ].astype(BF16)

    span = 2 * views * row_dev

    def grid_of(count):
        shape = (count * span, LANES)
        row = lax.broadcasted_iota(jnp.int32, shape, 0)
        col = lax.broadcasted_iota(jnp.int32, shape, 1)
        here = ((row // row_dev) % views == col // 16) & (
            (row // (views * row_dev)) % 2 == (col // 8) % 2
        )
        return row, col, here

    def weights(slot, row, slices, here):
        rows_past = (row % row_dev - slices * row_dev // z_dev).astype(F32)
        past = rows_past - (meta[slot, 0:1] + float((slot - 1) * row_dev)) - meta[slot, 8:9]
        return jnp.where(here, jnp.maximum(1.0 - jnp.abs(past), 0.0), 0.0)

    keep = 2 * views * z_dev
    row, col, here = grid_of(1)
    own = weights(1, row, col % z_dev, here)
    proj = dot(own[:, :keep].astype(BF16), sheared[...])

    for side, has in sides:
        @pl.when(has)
        def _():
            meta_copy(1 - side).wait_recv()

    row, col, here = grid_of(2)
    here = here & (row // span == (col // few) % 2)
    below = weights(0, row, col % few + few, here)
    above = weights(2, row, col % few, here)
    below_t = below.T[:keep].astype(BF16)
    above_t = above.T[:keep].astype(BF16)
    own_t = own.T[:keep].astype(BF16)
    for side, has in sides:
        @pl.when(has)
        def _():
            sheared_copy(1 - side).wait_recv()
    beside = dot(below[:, :keep].astype(BF16), sheared_in[0])
    beside += dot(above[:, :keep].astype(BF16), sheared_in[1])

    loads[1].wait()
    loads[2].wait()
    for h in range(2):
        for v in range(views):
            at = slice(h * half, (h + 1) * half)
            lo = (h * views + v) * row_dev
            here = proj[lo : lo + row_dev] + jnp.concatenate(
                [beside[lo : lo + row_dev], beside[span + lo : span + lo + row_dev]], axis=1
            )
            value = (ray[v, :, at] * (meas[v, :, at] - here)).astype(BF16)
            res[v, :, at] = value
            resid[lo : lo + row_dev] = value[:, :quarter]
            resid[span + lo : span + lo + row_dev] = value[:, quarter:]

    img_out[0] = dot(below_t, resid[...]).astype(BF16)
    img_out[1] = dot(above_t, resid[...]).astype(BF16)
    for side, has in sides:
        @pl.when(has)
        def _():
            image_copy(side).start()
    mine = jnp.concatenate([dot(own_t, resid[:span]), dot(own_t, resid[span:])], axis=1)
    for side, has in sides:
        @pl.when(has)
        def _():
            image_copy(1 - side).wait_recv()
    low_slices = lax.broadcasted_iota(jnp.int32, (z_dev, quarter), 0) < few
    for v in range(views):
        halves = []
        under = img_in[0, 16 * v : 16 * (v + 1)].astype(F32)
        over = img_in[1, 16 * v : 16 * (v + 1)].astype(F32)
        for h in range(2):
            x, y = under[8 * h : 8 * h + 8], over[8 * h : 8 * h + 8]
            added = jnp.concatenate(
                [jnp.where(low_slices, x, turn(y)), jnp.where(low_slices, turn(x), y)], axis=1
            )
            halves.append(mine[16 * v + 8 * h : 16 * v + 8 * h + 8] + added)
        put(images, v, halves[0], halves[1])

    def spread(k, _):
        dest = lax.rem(me + k, n_view)
        for l in range(2):
            y = 2 * dest + l
            total = jnp.zeros((blocks * 16, LANES), F32)
            for v in range(views):
                s = -shift[y, me * views + v] - 1
                total += dot(windows(images, v, s), taps_b[v * n_lines + y])
            total = total.astype(BF16)
            for b in range(blocks):
                back_out[dest, 16 * l : 16 * (l + 1), b * LANES : (b + 1) * LANES] = total[
                    16 * b : 16 * (b + 1)
                ]

        @pl.when(k < n_view)
        def _():
            rs_copy(k).start()

        return 0

    lax.fori_loop(1, n_view + 1, spread, 0)

    for l in range(2):
        for h in range(2):
            at = slice(h * half, (h + 1) * half)
            rows_at = slice(16 * l + 8 * h, 16 * l + 8 * h + 8)
            acc_at = back_out[me, 16 * l : 16 * l + 16].astype(F32)[8 * h : 8 * h + 8]
            upd[l, :, at] = acc_at

    def collect(k, _):
        src = lax.rem(me + k, n_view)
        rs_arrival(src).wait_recv()
        for l in range(2):
            part = back_in[src, 16 * l : 16 * l + 16].astype(F32)
            for h in range(2):
                at = slice(h * half, (h + 1) * half)
                upd[l, :, at] += part[8 * h : 8 * h + 8]
        return 0

    lax.fori_loop(1, n_view, collect, 0)
    loads[3].wait()
    upd[...] = vol[...] + vox[...] * upd[...]

    def drain(k, _):
        ag_copy(k).wait_send()
        rs_copy(k).wait_send()
        return 0

    lax.fori_loop(1, n_view, drain, 0)
    for side, has in sides:
        @pl.when(has)
        def _():
            meta_copy(side).wait_send()
            sheared_copy(side).wait_send()
            image_copy(side).wait_send()


def per_device(volume, vox_inv, measured, ray_inv, col_shift, col_frac, row_offset, row_frac):
    y_dev, z_dev, width = volume.shape
    row_dev, views = measured.shape[:2]
    n_view, n_slab = lax.axis_size("view"), lax.axis_size("slab")
    half = width // 2
    margin = (width // 8 // LANES + 1) * LANES
    n_lines = n_view * y_dev
    packed = 2 * views * z_dev
    vmem = pl.BlockSpec(memory_space=pltpu.VMEM)
    smem = pl.BlockSpec(memory_space=pltpu.SMEM)
    dma = pltpu.SemaphoreType.DMA
    sizes = (n_view, n_slab, views, z_dev, row_dev, width)
    upd, res = pl.pallas_call(
        functools.partial(kernel, sizes),
        out_shape=[
            jax.ShapeDtypeStruct(volume.shape, F32),
            jax.ShapeDtypeStruct((views, row_dev, width), BF16),
        ],
        in_specs=[pl.BlockSpec(memory_space=pltpu.HBM)] * 4 + [smem] * 4,
        out_specs=[vmem] * 2,
        scratch_shapes=[
            pltpu.VMEM(volume.shape, F32),
            pltpu.VMEM(volume.shape, F32),
            pltpu.VMEM((views, row_dev, width), F32),
            pltpu.VMEM((views, row_dev, width), F32),
            pltpu.VMEM((n_view, y_dev * z_dev, width), BF16),
            pltpu.VMEM((n_lines, (half + 2 * margin) // LANES, 2 * z_dev, LANES), BF16),
            pltpu.VMEM((views * n_lines, 2 * LANES, LANES), BF16),
            pltpu.VMEM((views * n_lines, 2 * LANES, LANES), BF16),
            pltpu.VMEM((views, half // LANES * 16, LANES), F32),
            pltpu.VMEM((packed, half), BF16),
            pltpu.VMEM((2, packed, half // 2), BF16),
            pltpu.VMEM((2, packed, half // 2), BF16),
            pltpu.VMEM((5, 16, LANES), F32),
            pltpu.VMEM((4 * views * row_dev, half // 2), BF16),
            pltpu.VMEM((2, packed, half // 2), BF16),
            pltpu.VMEM((2, packed, half // 2), BF16),
            pltpu.VMEM((views, (half + 2 * margin) // LANES, 2 * z_dev, LANES), BF16),
            pltpu.VMEM((n_view, 2 * y_dev * z_dev, half), BF16),
            pltpu.VMEM((n_view, 2 * y_dev * z_dev, half), BF16),
            dma((n_view,)), dma((n_view,)),
            dma((2,)), dma((2,)),
            dma((2,)), dma((2,)),
            dma((2,)), dma((2,)),
            dma((n_view,)), dma((n_view,)),
            dma((4,)),
        ],
        compiler_params=pltpu.CompilerParams(
            collective_id=0, has_side_effects=True, vmem_limit_bytes=63 * 1024 * 1024
        ),
    )(
        volume, vox_inv, measured.transpose(1, 0, 2), ray_inv.transpose(1, 0, 2),
        col_shift.T, col_frac.T, row_offset, row_frac,
    )
    return upd, res.transpose(1, 0, 2)


def solution(mesh):
    in_specs = (
        P("view", "slab", None),
        P("view", "slab", None),
        P("slab", "view", None),
        P("slab", "view", None),
        P(),
        P(),
        P("view", "slab"),
        P("view", "slab"),
    )
    out_specs = (P("view", "slab", None), P("slab", "view", None))
    return jax.shard_map(
        per_device, mesh=mesh, in_specs=in_specs, out_specs=out_specs, check_vma=False
    )
```

```python
import functools

import jax
import jax.numpy as jnp
from jax import lax
from jax.experimental import pallas as pl
from jax.experimental.pallas import tpu as pltpu
from jax.sharding import PartitionSpec as P

F32 = jnp.float32
BF16 = jnp.bfloat16
LANES = 128


def dot(a, b):
    return jnp.dot(a, b, preferred_element_type=F32)


def kernel(
    sizes, vol_at, vox_at, meas_at, ray_at, shift, frac, off, rfrac, upd, res,
    vol, vox, meas, ray,
    gat, lines, taps_f, taps_b, acc, sheared, sheared_out, sheared_in, meta, resid, img_out, img_in, images, back_out, back_in,
    ag_send, ag_recv, me_send, me_recv, sh_send, sh_recv, im_send, im_recv, rs_send, rs_recv, load_sem,
):
    n_view, n_slab, views, z_dev, row_dev, width = sizes
    half = width // 2
    margin = (lines.shape[1] * LANES - half) // 2
    blocks = half // LANES
    quarter = half // 2
    n_lines = 2 * n_view
    me = lax.axis_index("view")
    slab = lax.axis_index("slab")
    has_lo = slab > 0
    has_hi = slab < n_slab - 1

    loads = [
        pltpu.make_async_copy(src, dst, load_sem.at[i])
        for i, (src, dst) in enumerate(((vol_at, vol), (meas_at, meas), (ray_at, ray), (vox_at, vox)))
    ]
    loads[0].start()

    def peer(k):
        return lax.rem(jnp.where(2 * me < n_view, me + k, me + n_view - k), n_view)

    inner = (me > 0) & (me < n_view - 1) & (n_view == 4)

    def handed_on(k):
        return inner & (k == 2)

    def ag_copy(k):
        dest = peer(k)
        return pltpu.make_async_remote_copy(
            gat.at[me], gat.at[me], ag_send.at[k], ag_recv.at[me], device_id={"view": dest}
        )

    def ag_forward():
        src = peer(1)
        return pltpu.make_async_remote_copy(
            gat.at[src], gat.at[src], ag_send.at[0], ag_recv.at[src], device_id={"view": 2 * me - src}
        )

    def ag_arrival(src):
        return pltpu.make_async_remote_copy(
            gat.at[src], gat.at[src], ag_send.at[0], ag_recv.at[src], device_id={"view": src}
        )

    def rs_copy(k):
        dest = peer(k)
        return pltpu.make_async_remote_copy(
            back_out.at[dest], back_in.at[me], rs_send.at[k], rs_recv.at[me], device_id={"view": dest}
        )

    def rs_arrival(src):
        return pltpu.make_async_remote_copy(
            back_out.at[src], back_in.at[src], rs_send.at[0], rs_recv.at[src], device_id={"view": src}
        )

    def halo(own, slots, send, recv, side, low_slot, high_slot):
        slot = high_slot if side == 0 else low_slot
        return pltpu.make_async_remote_copy(
            own, slots.at[slot], send.at[side], recv.at[1 - side],
            device_id={"slab": slab - 1 if side == 0 else slab + 1},
        )

    sides = ((0, has_lo), (1, has_hi))

    def meta_copy(side):
        return halo(meta.at[3 + side], meta, me_send, me_recv, side, 0, 2)

    def sheared_copy(side):
        return halo(sheared_out.at[side], sheared_in, sh_send, sh_recv, side, 0, 1)

    def image_copy(side):
        return halo(img_out.at[side], img_in, im_send, im_recv, side, 0, 1)

    barrier = pltpu.get_barrier_semaphore()

    def greet(k, _):
        pl.semaphore_signal(barrier, inc=1, device_id={"view": lax.rem(me + k, n_view)})
        return 0

    lax.fori_loop(1, n_view, greet, 0)
    for side, has in sides:
        @pl.when(has)
        def _():
            pl.semaphore_signal(barrier, inc=1, device_id={"slab": slab - 1 if side == 0 else slab + 1})

    loads[0].wait()
    gat[me] = vol[...].reshape(2 * z_dev, width).astype(BF16)

    lane = lax.broadcasted_iota(jnp.int32, (8, LANES), 1)
    few = z_dev // 2
    slice_of = {1: lane % z_dev, 3: lane % few, 4: lane % few + few}
    for slot, slices in slice_of.items():
        offs = jnp.zeros((8, LANES), F32)
        fracs = jnp.zeros((8, LANES), F32)
        for v in range(views):
            for z in range(z_dev):
                here = (lane // 16 == v) & (slices == z)
                offs = jnp.where(here, off[v, z].astype(F32), offs)
                fracs = jnp.where(here, rfrac[v, z], fracs)
        meta[slot, 0:8] = offs
        meta[slot, 8:16] = fracs

    peers = n_view + 1 - (slab == 0).astype(jnp.int32) - (slab == n_slab - 1).astype(jnp.int32)
    pl.semaphore_wait(barrier, peers)

    def send_lines(k, _):
        @pl.when(jnp.logical_not(handed_on(k)))
        def _():
            ag_copy(k).start()

        return 0

    lax.fori_loop(1, n_view, send_lines, 0)
    for load in loads[1:]:
        load.start()
    for side, has in sides:
        @pl.when(has)
        def _():
            meta_copy(side).start()

        @pl.when(jnp.logical_not(has))
        def _():
            slot = 0 if side == 0 else 2
            meta[slot] = jnp.zeros(meta.shape[1:], F32)
            sheared_in[side] = jnp.zeros(sheared_in.shape[1:], BF16)
            img_in[side] = jnp.zeros(img_in.shape[1:], BF16)

    delta = lax.broadcasted_iota(jnp.int32, (2 * LANES, LANES), 0) - lax.broadcasted_iota(
        jnp.int32, (2 * LANES, LANES), 1
    )

    def place(s):
        whole = lax.shift_right_arithmetic(s, 7)
        return whole, s - whole * LANES

    def taps(s, first, second):
        _, r = place(s)
        return jnp.where(delta == r, first, jnp.where(delta == r + 1, second, 0.0)).astype(BF16)

    def build(y, _):
        for v in range(views):
            s = shift[y, me * views + v]
            f = frac[y, me * views + v]
            taps_f[v * n_lines + y] = taps(s, 1.0 - f, f)
            taps_b[v * n_lines + y] = taps(-s - 1, f, 1.0 - f)
        return 0

    lax.fori_loop(0, n_lines, build, 0)

    def put(ref, at, low, high):
        zeros = jnp.zeros((z_dev, margin), F32)
        top = jnp.concatenate([zeros, low, high[:, :margin]], axis=1)
        bottom = jnp.concatenate([low[:, half - margin :], high, zeros], axis=1)
        both = jnp.concatenate([top, bottom], axis=0).astype(BF16)
        for b in range(both.shape[1] // LANES):
            ref[at, b] = both[:, b * LANES : (b + 1) * LANES]

    def windows(ref, at, s):
        whole, _ = place(s)
        taken = ref[at, pl.ds(margin // LANES + whole, blocks + 1)]
        taken = taken.reshape((blocks + 1) * 16, LANES)
        return jnp.concatenate([taken[:-16], taken[16:]], axis=1)

    acc[...] = jnp.zeros(acc.shape, F32)

    def project(k, _):
        src = peer(k)

        @pl.when(k > 0)
        def _():
            ag_arrival(src).wait_recv()

        @pl.when(inner & (k == 1))
        def _():
            ag_forward().start()

        for l in range(2):
            y = 2 * src + l
            x = gat[src].astype(F32)[l * z_dev : (l + 1) * z_dev]
            put(lines, y, x[:, :half], x[:, half:])
            for v in range(views):
                s = shift[y, me * views + v]
                acc[v] += dot(windows(lines, y, s), taps_f[v * n_lines + y])
        return 0

    lax.fori_loop(0, n_view, project, 0)
    low_rows = lax.broadcasted_iota(jnp.int32, (z_dev, LANES), 0) < few

    def turn(x):
        return pltpu.roll(x, few, 0)

    for v in range(views):
        for b in range(blocks // 2):
            first = acc[v, 16 * b : 16 * (b + 1)]
            second = acc[v, 16 * (b + blocks // 2) : 16 * (b + blocks // 2 + 1)]
            down, up = [], []
            for h in range(2):
                x, y = first[8 * h : 8 * h + 8], second[8 * h : 8 * h + 8]
                down.append(jnp.where(low_rows, x, turn(y)))
                up.append(jnp.where(low_rows, turn(x), y))
            at = (slice(16 * v, 16 * (v + 1)), slice(b * LANES, (b + 1) * LANES))
            sheared_out[(0,) + at] = jnp.concatenate(down, axis=0).astype(BF16)
            sheared_out[(1,) + at] = jnp.concatenate(up, axis=0).astype(BF16)

    for side, has in sides:
        @pl.when(has)
        def _():
            sheared_copy(side).start()

    for v in range(views):
        for b in range(blocks):
            sheared[16 * v : 16 * (v + 1), b * LANES : (b + 1) * LANES] = acc[
                v, 16 * b : 16 * (b + 1)
            ].astype(BF16)

    span = 2 * views * row_dev

    def grid_of(count):
        shape = (count * span, LANES)
        row = lax.broadcasted_iota(jnp.int32, shape, 0)
        col = lax.broadcasted_iota(jnp.int32, shape, 1)
        here = ((row // row_dev) % views == col // 16) & (
            (row // (views * row_dev)) % 2 == (col // 8) % 2
        )
        return row, col, here

    def weights(slot, row, slices, here):
        rows_past = (row % row_dev - slices * row_dev // z_dev).astype(F32)
        past = rows_past - (meta[slot, 0:1] + float((slot - 1) * row_dev)) - meta[slot, 8:9]
        return jnp.where(here, jnp.maximum(1.0 - jnp.abs(past), 0.0), 0.0)

    keep = 2 * views * z_dev
    row, col, here = grid_of(1)
    own = weights(1, row, col % z_dev, here)
    proj = dot(own[:, :keep].astype(BF16), sheared[...])

    for side, has in sides:
        @pl.when(has)
        def _():
            meta_copy(1 - side).wait_recv()

    row, col, here = grid_of(2)
    here = here & (row // span == (col // few) % 2)
    below = weights(0, row, col % few + few, here)
    above = weights(2, row, col % few, here)
    below_t = below.T[:keep].astype(BF16)
    above_t = above.T[:keep].astype(BF16)
    own_t = own.T[:keep].astype(BF16)
    for side, has in sides:
        @pl.when(has)
        def _():
            sheared_copy(1 - side).wait_recv()
    beside = dot(below[:, :keep].astype(BF16), sheared_in[0])
    beside += dot(above[:, :keep].astype(BF16), sheared_in[1])

    loads[1].wait()
    loads[2].wait()
    for h in range(2):
        for v in range(views):
            at = slice(h * half, (h + 1) * half)
            lo = (h * views + v) * row_dev
            here = proj[lo : lo + row_dev] + jnp.concatenate(
                [beside[lo : lo + row_dev], beside[span + lo : span + lo + row_dev]], axis=1
            )
            value = (ray[v, :, at] * (meas[v, :, at] - here)).astype(BF16)
            res[v, :, at] = value
            resid[lo : lo + row_dev] = value[:, :quarter]
            resid[span + lo : span + lo + row_dev] = value[:, quarter:]

    img_out[0] = dot(below_t, resid[...]).astype(BF16)
    img_out[1] = dot(above_t, resid[...]).astype(BF16)
    for side, has in sides:
        @pl.when(has)
        def _():
            image_copy(side).start()
    mine = jnp.concatenate([dot(own_t, resid[:span]), dot(own_t, resid[span:])], axis=1)
    for side, has in sides:
        @pl.when(has)
        def _():
            image_copy(1 - side).wait_recv()
    low_slices = lax.broadcasted_iota(jnp.int32, (z_dev, quarter), 0) < few
    for v in range(views):
        halves = []
        under = img_in[0, 16 * v : 16 * (v + 1)].astype(F32)
        over = img_in[1, 16 * v : 16 * (v + 1)].astype(F32)
        for h in range(2):
            x, y = under[8 * h : 8 * h + 8], over[8 * h : 8 * h + 8]
            added = jnp.concatenate(
                [jnp.where(low_slices, x, turn(y)), jnp.where(low_slices, turn(x), y)], axis=1
            )
            halves.append(mine[16 * v + 8 * h : 16 * v + 8 * h + 8] + added)
        put(images, v, halves[0], halves[1])

    def spread(i, _):
        k = n_view - i
        dest = peer(k)
        for l in range(2):
            y = 2 * dest + l
            total = jnp.zeros((blocks * 16, LANES), F32)
            for v in range(views):
                s = -shift[y, me * views + v] - 1
                total += dot(windows(images, v, s), taps_b[v * n_lines + y])
            total = total.astype(BF16)
            for b in range(blocks):
                back_out[dest, 16 * l : 16 * (l + 1), b * LANES : (b + 1) * LANES] = total[
                    16 * b : 16 * (b + 1)
                ]

        @pl.when(k > 0)
        def _():
            rs_copy(k).start()

        return 0

    lax.fori_loop(1, n_view + 1, spread, 0)

    for l in range(2):
        for h in range(2):
            at = slice(h * half, (h + 1) * half)
            rows_at = slice(16 * l + 8 * h, 16 * l + 8 * h + 8)
            acc_at = back_out[me, 16 * l : 16 * l + 16].astype(F32)[8 * h : 8 * h + 8]
            upd[l, :, at] = acc_at

    def collect(k, _):
        src = peer(k)
        rs_arrival(src).wait_recv()
        for l in range(2):
            part = back_in[src, 16 * l : 16 * l + 16].astype(F32)
            for h in range(2):
                at = slice(h * half, (h + 1) * half)
                upd[l, :, at] += part[8 * h : 8 * h + 8]
        return 0

    lax.fori_loop(1, n_view, collect, 0)
    loads[3].wait()
    upd[...] = vol[...] + vox[...] * upd[...]

    def drain(k, _):
        @pl.when(jnp.logical_not(handed_on(k)))
        def _():
            ag_copy(k).wait_send()

        rs_copy(k).wait_send()
        return 0

    lax.fori_loop(1, n_view, drain, 0)

    @pl.when(inner)
    def _():
        ag_forward().wait_send()

    for side, has in sides:
        @pl.when(has)
        def _():
            meta_copy(side).wait_send()
            sheared_copy(side).wait_send()
            image_copy(side).wait_send()


def per_device(volume, vox_inv, measured, ray_inv, col_shift, col_frac, row_offset, row_frac):
    y_dev, z_dev, width = volume.shape
    row_dev, views = measured.shape[:2]
    n_view, n_slab = lax.axis_size("view"), lax.axis_size("slab")
    half = width // 2
    margin = (width // 8 // LANES + 1) * LANES
    n_lines = n_view * y_dev
    packed = 2 * views * z_dev
    vmem = pl.BlockSpec(memory_space=pltpu.VMEM)
    smem = pl.BlockSpec(memory_space=pltpu.SMEM)
    dma = pltpu.SemaphoreType.DMA
    sizes = (n_view, n_slab, views, z_dev, row_dev, width)
    upd, res = pl.pallas_call(
        functools.partial(kernel, sizes),
        out_shape=[
            jax.ShapeDtypeStruct(volume.shape, F32),
            jax.ShapeDtypeStruct((views, row_dev, width), BF16),
        ],
        in_specs=[pl.BlockSpec(memory_space=pltpu.HBM)] * 4 + [smem] * 4,
        out_specs=[vmem] * 2,
        scratch_shapes=[
            pltpu.VMEM(volume.shape, F32),
            pltpu.VMEM(volume.shape, F32),
            pltpu.VMEM((views, row_dev, width), F32),
            pltpu.VMEM((views, row_dev, width), F32),
            pltpu.VMEM((n_view, y_dev * z_dev, width), BF16),
            pltpu.VMEM((n_lines, (half + 2 * margin) // LANES, 2 * z_dev, LANES), BF16),
            pltpu.VMEM((views * n_lines, 2 * LANES, LANES), BF16),
            pltpu.VMEM((views * n_lines, 2 * LANES, LANES), BF16),
            pltpu.VMEM((views, half // LANES * 16, LANES), F32),
            pltpu.VMEM((packed, half), BF16),
            pltpu.VMEM((2, packed, half // 2), BF16),
            pltpu.VMEM((2, packed, half // 2), BF16),
            pltpu.VMEM((5, 16, LANES), F32),
            pltpu.VMEM((4 * views * row_dev, half // 2), BF16),
            pltpu.VMEM((2, packed, half // 2), BF16),
            pltpu.VMEM((2, packed, half // 2), BF16),
            pltpu.VMEM((views, (half + 2 * margin) // LANES, 2 * z_dev, LANES), BF16),
            pltpu.VMEM((n_view, 2 * y_dev * z_dev, half), BF16),
            pltpu.VMEM((n_view, 2 * y_dev * z_dev, half), BF16),
            dma((n_view,)), dma((n_view,)),
            dma((2,)), dma((2,)),
            dma((2,)), dma((2,)),
            dma((2,)), dma((2,)),
            dma((n_view,)), dma((n_view,)),
            dma((4,)),
        ],
        compiler_params=pltpu.CompilerParams(
            collective_id=0, has_side_effects=True, vmem_limit_bytes=63 * 1024 * 1024
        ),
    )(
        volume, vox_inv, measured.transpose(1, 0, 2), ray_inv.transpose(1, 0, 2),
        col_shift.T, col_frac.T, row_offset, row_frac,
    )
    return upd, res.transpose(1, 0, 2)


def solution(mesh):
    in_specs = (
        P("view", "slab", None),
        P("view", "slab", None),
        P("slab", "view", None),
        P("slab", "view", None),
        P(),
        P(),
        P("view", "slab"),
        P("view", "slab"),
    )
    out_specs = (P("view", "slab", None), P("slab", "view", None))
    return jax.shard_map(
        per_device, mesh=mesh, in_specs=in_specs, out_specs=out_specs, check_vma=False
    )
```
